32 devices in a mesh: ctx: 8 (over z, y), head: 4 (over x, core).
Axes of the slice: x: 2, y: 2, z: 4, core: 2. Of those that a mesh axis runs over, the one named last changes fastest.
Arguments:
- queries: bfloat16 [1024, 4096], P(('ctx', 'head')), may hold values from -8 to 8
- key_rows: bfloat16 [1024, 512], P(('ctx', 'head')), may hold values from -8 to 8
- value_matrix: bfloat16 [1024, 512], P(('ctx', 'head')), may hold values from -6 to 6
- output_gradient: bfloat16 [1024, 4096], P(('ctx', 'head')), may hold values from -6 to 6
- doc_lengths: int32 [4], replicated, may hold values from 1 to 384, as said below
Outputs:
- attended: bfloat16 [1024, 4096], P(('ctx', 'head'))
- log_norm: float32 [32, 1024], P('head', 'ctx')
- grad_queries: bfloat16 [1024, 4096], P(('ctx', 'head'))
- grad_keys: bfloat16 [1024, 512], P(('ctx', 'head'))
- grad_values: bfloat16 [1024, 512], P(('ctx', 'head'))
The draws below stay inside these ranges and needn't reach their ends.
Inputs may be any that keep to these rules, and one draw needn't show every extreme that they name: `doc_lengths`: 4 document lengths in order; they sum to 1024, and the longest is exactly 384.
All inputs are finite; a program needn't handle non-finite values.
Results may differ from the reference program's by a relative error of at most 0.017.
Values may be sent and summed in bfloat16 or wider, within the bound.
A program may use at most 64 MiB of HBM per device.

```python
import math
import jax
import jax.numpy as jnp
from jax import lax

QUERY_HEADS = 32
KEY_VALUE_HEADS = 4
HEAD_WIDTH = 128
PACKED_LENGTH = 1024
LONGEST_DOC_LEN = 384
NDOC = 4


def draw_queries(key, part):
    key = jax.random.fold_in(key, 11)
    start_offset = jax.random.truncated_normal(key, -8.0, 8.0, (PACKED_LENGTH, QUERY_HEADS, HEAD_WIDTH), jnp.float32)
    return start_offset.reshape(PACKED_LENGTH, QUERY_HEADS * HEAD_WIDTH).astype(jnp.bfloat16)


def draw_key_rows(key, part):
    key = jax.random.fold_in(key, 12)
    start_offset = jax.random.truncated_normal(key, -8.0, 8.0, (PACKED_LENGTH, KEY_VALUE_HEADS, HEAD_WIDTH), jnp.float32)
    return start_offset.reshape(PACKED_LENGTH, KEY_VALUE_HEADS * HEAD_WIDTH).astype(jnp.bfloat16)


def draw_doc_lengths(key, part):
    key = jax.random.fold_in(key, 13)
    others = NDOC - 1
    remainder = PACKED_LENGTH - LONGEST_DOC_LEN
    places = jnp.arange(others, dtype=jnp.int32)
    lengths_now = (remainder // others + (places < remainder % others).astype(jnp.int32)).astype(jnp.int32)
    half_count = others // 2
    for round_idx in range(8):
        order_key, amount_key = jax.random.split(jax.random.fold_in(key, round_idx + 1))
        order = jax.random.permutation(order_key, others).astype(jnp.int32)
        first = order[:half_count]
        second = order[half_count:2 * half_count]
        first_len = lengths_now[first]
        second_len = lengths_now[second]
        lower = -jnp.minimum(first_len - 1, LONGEST_DOC_LEN - second_len)
        upper = jnp.minimum(second_len - 1, LONGEST_DOC_LEN - first_len) + 1
        moved = jax.random.randint(amount_key, (half_count,), lower, upper).astype(jnp.int32)
        lengths_now = lengths_now.at[first].add(moved).at[second].add(-moved)
    spot_key = jax.random.fold_in(key, 99)
    spot = jax.random.randint(spot_key, (), 0, NDOC).astype(jnp.int32)
    indices = jnp.arange(NDOC, dtype=jnp.int32)
    before = lengths_now[jnp.clip(indices, 0, others - 1)]
    after = lengths_now[jnp.clip(indices - 1, 0, others - 1)]
    result = jnp.where(indices < spot, before, jnp.where(indices == spot, LONGEST_DOC_LEN, after))
    return result.astype(jnp.int32)


def shard_levels(rng, extent, cuts, least, top_value):
    gain, own = 1.0, jax.random.fold_in(rng, 6)
    for position, parts in cuts:
        draws = jnp.exp(jax.random.uniform(jax.random.fold_in(own, position), (parts,), jnp.float32, least / len(cuts), top_value / len(cuts)))
        gain = gain * jnp.repeat(draws, extent[position] // parts).reshape([-1 if axis == position else 1 for axis in range(len(extent))])
    return gain


def normal_values(key, shape, deviation, bound, cuts=(), kind=jnp.bfloat16):
    values = jax.random.normal(key, shape, jnp.float32) * deviation
    if len(cuts) > 0:
        values = shard_levels(key, shape, cuts, -0.22, 0.18) * values
    return jnp.clip(values, min=-bound, max=bound).astype(kind)


def setup_inputs(seed: int = 0) -> dict:
    seeds = jax.random.split(jax.random.key(seed), 6)
    queries = draw_queries(jax.random.fold_in(seeds[5], 71), 0)
    key_rows = draw_key_rows(jax.random.fold_in(seeds[5], 71), 0)
    value_matrix = normal_values(seeds[2], (PACKED_LENGTH, KEY_VALUE_HEADS * HEAD_WIDTH), 1.0, 6.0, ((0, 32),))
    output_gradient = normal_values(seeds[3], (PACKED_LENGTH, QUERY_HEADS * HEAD_WIDTH), 1.0, 6.0, ((0, 32),))
    doc_lengths = draw_doc_lengths(jax.random.fold_in(seeds[5], 71), 0)
    return {"queries": queries, "key_rows": key_rows, "value_matrix": value_matrix, "output_gradient": output_gradient, "doc_lengths": doc_lengths}


neg_fill = -1e+30

def doc_numbers(positions, doc_lengths):
    bounds = jnp.cumsum(doc_lengths).astype(jnp.int32)
    counted = lax.optimization_barrier(jnp.sum((positions[:, None] >= bounds[None, :]).astype(jnp.int32), axis=1)).astype(jnp.int32)
    return jnp.where(positions >= 0, counted, -1).astype(jnp.int32)

def reference(queries, key_rows, value_matrix, output_gradient, doc_lengths):
    score_scale = 1.0 / math.sqrt(HEAD_WIDTH)
    group_width = QUERY_HEADS // KEY_VALUE_HEADS
    extent_length = math.gcd(512, PACKED_LENGTH)
    key_extent = LONGEST_DOC_LEN + extent_length
    filler_length = jnp.zeros((LONGEST_DOC_LEN, KEY_VALUE_HEADS * HEAD_WIDTH), jnp.bfloat16)
    padded_key_rows = jnp.concatenate([filler_length, key_rows], axis=0)
    padded_value_rows = jnp.concatenate([filler_length, value_matrix], axis=0)
    positions = jnp.arange(PACKED_LENGTH + LONGEST_DOC_LEN, dtype=jnp.int32) - LONGEST_DOC_LEN
    documents = doc_numbers(positions, doc_lengths)

    def one_block(sums_in, block_idx):
        grad_keys_acc, grad_values_acc = sums_in
        leading_row = (block_idx * extent_length).astype(jnp.int32)
        block_of_queries = lax.dynamic_slice_in_dim(queries, leading_row, extent_length, 0).astype(jnp.float32).reshape(extent_length, KEY_VALUE_HEADS, group_width, HEAD_WIDTH)
        block_gradient = lax.dynamic_slice_in_dim(output_gradient, leading_row, extent_length, 0).astype(jnp.float32).reshape(extent_length, KEY_VALUE_HEADS, group_width, HEAD_WIDTH)
        block_of_keys = lax.dynamic_slice_in_dim(padded_key_rows, leading_row, key_extent, 0).astype(jnp.float32).reshape(key_extent, KEY_VALUE_HEADS, HEAD_WIDTH)
        block_of_values = lax.dynamic_slice_in_dim(padded_value_rows, leading_row, key_extent, 0).astype(jnp.float32).reshape(key_extent, KEY_VALUE_HEADS, HEAD_WIDTH)
        query_pos = lax.dynamic_slice_in_dim(positions, leading_row + LONGEST_DOC_LEN, extent_length, 0)
        key_pos = lax.dynamic_slice_in_dim(positions, leading_row, key_extent, 0)
        query_doc = lax.dynamic_slice_in_dim(documents, leading_row + LONGEST_DOC_LEN, extent_length, 0)
        key_doc = lax.dynamic_slice_in_dim(documents, leading_row, key_extent, 0)
        visible = (query_doc[:, None] == key_doc[None, :]) & (key_pos[None, :] <= query_pos[:, None])
        scores = jnp.einsum('pgjd,kgd->gjpk', block_of_queries, block_of_keys) * score_scale
        row_max = lax.optimization_barrier(jnp.max(jnp.where(visible, scores, neg_fill), axis=3))
        row_sum = lax.optimization_barrier(jnp.sum(jnp.where(visible, jnp.exp(scores - row_max[..., None]), 0.0), axis=3))
        log_total = row_max + jnp.log(row_sum)
        probabilities = jnp.where(visible, jnp.exp(scores - log_total[..., None]), 0.0).astype(jnp.bfloat16)
        probabilities = lax.optimization_barrier(probabilities).astype(jnp.float32)
        attended = jnp.einsum('gjpk,kgd->pgjd', probabilities, block_of_values).astype(jnp.bfloat16)
        row_delta = jnp.einsum('pgjd,pgjd->gjp', block_gradient, attended.astype(jnp.float32))
        grad_probs = jnp.einsum('pgjd,kgd->gjpk', block_gradient, block_of_values)
        score_gradient = (probabilities * (grad_probs - row_delta[..., None]) * score_scale).astype(jnp.bfloat16)
        score_gradient = lax.optimization_barrier(score_gradient).astype(jnp.float32)
        grad_query = jnp.einsum('gjpk,kgd->pgjd', score_gradient, block_of_keys).astype(jnp.bfloat16)
        key_summands = jnp.einsum('urzm,zura->mua', score_gradient, block_of_queries).reshape(key_extent, KEY_VALUE_HEADS * HEAD_WIDTH)
        value_summands = jnp.einsum('urzm,zura->mua', probabilities, block_gradient).reshape(key_extent, KEY_VALUE_HEADS * HEAD_WIDTH)
        grad_keys_acc = lax.dynamic_update_slice_in_dim(grad_keys_acc, lax.dynamic_slice_in_dim(grad_keys_acc, leading_row, key_extent, 0) + key_summands, leading_row, 0)
        grad_values_acc = lax.dynamic_update_slice_in_dim(grad_values_acc, lax.dynamic_slice_in_dim(grad_values_acc, leading_row, key_extent, 0) + value_summands, leading_row, 0)
        return ((grad_keys_acc, grad_values_acc), (attended.reshape(extent_length, QUERY_HEADS * HEAD_WIDTH), log_total.reshape(QUERY_HEADS, extent_length), grad_query.reshape(extent_length, QUERY_HEADS * HEAD_WIDTH)))
    vanishing_sums = jnp.zeros((PACKED_LENGTH + LONGEST_DOC_LEN, KEY_VALUE_HEADS * HEAD_WIDTH), jnp.float32)
    (grad_keys_acc, grad_values_acc), (outputs, totals, query_grads) = lax.scan(one_block, (vanishing_sums, vanishing_sums), jnp.arange(PACKED_LENGTH // extent_length, dtype=jnp.int32))
    attended = outputs.reshape(PACKED_LENGTH, QUERY_HEADS * HEAD_WIDTH)
    log_norm = jnp.transpose(totals, (1, 0, 2)).reshape(QUERY_HEADS, PACKED_LENGTH)
    grad_queries = query_grads.reshape(PACKED_LENGTH, QUERY_HEADS * HEAD_WIDTH)
    grad_keys = grad_keys_acc[LONGEST_DOC_LEN:].astype(jnp.bfloat16)
    grad_values = grad_values_acc[LONGEST_DOC_LEN:].astype(jnp.bfloat16)
    return (attended, log_norm, grad_queries, grad_keys, grad_values)
```

```python
import functools
import math

import jax
import jax.numpy as jnp
from jax import lax
from jax.experimental import pallas as pl
from jax.experimental.pallas import tpu as pltpu
from jax.sharding import PartitionSpec as P

WIDTH = 128
MESH = pl.DeviceIdType.MESH
FILL = -1e30
NT = (((1,), (1,)), ((), ()))
TN = (((0,), (0,)), ((), ()))
NN = (((1,), (0,)), ((), ()))


def dot(a, b, dims):
    return lax.dot_general(a, b, dims, preferred_element_type=jnp.float32)


def kernel(
    ctxs,
    heads,
    reach,
    q_ref,
    k_ref,
    v_ref,
    g_ref,
    doc_ref,
    att_out,
    norm_out,
    dq_out,
    dk_out,
    dv_out,
    q_buf,
    g_buf,
    kv_buf,
    bias,
    probs,
    dscores,
    att_buf,
    dq_buf,
    dkv_own,
    dkv_send,
    dkv_recv,
    dkv_fin,
    norm_buf,
    in_send,
    in_recv,
    ctx_send,
    ctx_recv,
    out_send,
    out_recv,
    back_send,
    back_recv,
    local_sem,
):
    u = lax.axis_index("ctx")
    g = lax.axis_index("head")
    tok = q_ref.shape[0]
    block = tok * heads
    group_cols = q_ref.shape[1] // heads
    per_group = group_cols // WIDTH
    window = reach * block
    scale = 1.0 / math.sqrt(WIDTH)
    last = reach - 1

    def rows(i):
        return pl.ds(pl.multiple_of(i * tok, tok), tok)

    def cols(i, width):
        return pl.ds(pl.multiple_of(i * width, width), width)

    barrier = pltpu.get_barrier_semaphore()
    for d in range(1, heads):
        pl.semaphore_signal(
            barrier, inc=1, device_id=(u, lax.rem(g + d, heads)), device_id_type=MESH
        )
    for k in range(1, reach):
        @pl.when(u + k < ctxs)
        def _():
            pl.semaphore_signal(barrier, inc=1, device_id=(u + k, g), device_id_type=MESH)

        @pl.when(u - k >= 0)
        def _():
            pl.semaphore_signal(barrier, inc=1, device_id=(u - k, g), device_id_type=MESH)

    own = [
        (k_ref.at[:, cols(g, WIDTH)], kv_buf.at[last, rows(g), pl.ds(0, WIDTH)]),
        (v_ref.at[:, cols(g, WIDTH)], kv_buf.at[last, rows(g), pl.ds(WIDTH, WIDTH)]),
        (q_ref.at[:, cols(g, group_cols)], q_buf.at[rows(g), :]),
        (g_ref.at[:, cols(g, group_cols)], g_buf.at[rows(g), :]),
    ]
    own_copies = [
        pltpu.make_async_copy(src, dst, local_sem.at[i]) for i, (src, dst) in enumerate(own)
    ]
    for copy in own_copies:
        copy.start()

    for k in range(1, reach):
        @pl.when(u - k < 0)
        def _():
            kv_buf[last - k] = jnp.zeros((block, 2 * WIDTH), jnp.bfloat16)

        @pl.when(u + k >= ctxs)
        def _():
            dkv_recv[k - 1] = jnp.zeros((block, 2 * WIDTH), jnp.bfloat16)

    pl.semaphore_wait(
        barrier,
        (heads - 1) + jnp.minimum(u, reach - 1) + jnp.minimum(ctxs - 1 - u, reach - 1),
    )

    def in_src(kind, i):
        ref = (k_ref, v_ref, q_ref, g_ref)[kind]
        return ref.at[:, cols(i, WIDTH if kind < 2 else group_cols)]

    def in_dst(kind, i):
        if kind < 2:
            return kv_buf.at[last, rows(i), pl.ds(kind * WIDTH, WIDTH)]
        return (q_buf, g_buf)[kind - 2].at[rows(i), :]

    def in_copy(kind, d):
        peer = lax.rem(g + d, heads)
        return pltpu.make_async_remote_copy(
            src_ref=in_src(kind, peer),
            dst_ref=in_dst(kind, g),
            send_sem=in_send.at[kind, d - 1],
            recv_sem=in_recv.at[kind, d - 1],
            device_id=(u, peer),
            device_id_type=MESH,
        )

    def in_arrival(kind, d):
        peer = lax.rem(g + heads - d, heads)
        return pltpu.make_async_remote_copy(
            src_ref=in_dst(kind, peer),
            dst_ref=in_dst(kind, peer),
            send_sem=in_send.at[kind, d - 1],
            recv_sem=in_recv.at[kind, d - 1],
            device_id=(u, peer),
            device_id_type=MESH,
        )

    for kind in range(4):
        for d in range(1, heads):
            in_copy(kind, d).start()

    query_pos = u * block + lax.broadcasted_iota(jnp.int32, (1, block), 1)
    begins = jnp.zeros((1, block), jnp.int32)
    bound = jnp.int32(0)
    for j in range(doc_ref.shape[0]):
        bound = bound + doc_ref[j]
        begins = jnp.where(query_pos >= bound, bound, begins)
    key_pos = (u - last) * block + lax.broadcasted_iota(jnp.int32, (window, block), 0)
    bias[...] = jnp.where((key_pos >= begins) & (key_pos <= query_pos), 0.0, FILL)

    own_copies[0].wait()
    own_copies[1].wait()
    for kind in range(2):
        for d in range(1, heads):
            in_arrival(kind, d).wait_recv()

    def ctx_copy(k, to):
        return pltpu.make_async_remote_copy(
            src_ref=kv_buf.at[last],
            dst_ref=kv_buf.at[last - k],
            send_sem=ctx_send.at[k - 1],
            recv_sem=ctx_recv.at[k - 1],
            device_id=(to, g),
            device_id_type=MESH,
        )

    for k in range(1, reach):
        @pl.when(u + k < ctxs)
        def _():
            ctx_copy(k, u + k).start()

    own_copies[2].wait()
    for d in range(1, heads):
        in_arrival(2, d).wait_recv()
    for k in range(1, reach):
        @pl.when(u - k >= 0)
        def _():
            ctx_copy(k, u - k).wait_recv()

    keys = kv_buf[:, :, :WIDTH].reshape(window, WIDTH)
    values = kv_buf[:, :, WIDTH:].reshape(window, WIDTH)

    factor = scale * math.log2(math.e)
    for h in range(per_group):
        at = slice(h * WIDTH, (h + 1) * WIDTH)
        scores = dot(keys, q_buf[:, at], NT) + bias[...]
        top = jnp.max(scores, axis=0, keepdims=True)
        weights = jnp.exp2((scores - top) * factor)
        total = jnp.sum(weights, axis=0, keepdims=True)
        norm_buf[h : h + 1, :] = top * scale + jnp.log(total)
        p = (weights * (1.0 / total)).astype(jnp.bfloat16)
        probs[:, h * block : (h + 1) * block] = p
        att_buf[:, at] = dot(p, values, TN).astype(jnp.bfloat16)

    def out_src(kind, i):
        if kind < 2:
            return (att_buf, dq_buf)[kind].at[rows(i), :]
        return dkv_fin.at[rows(i), pl.ds((kind - 2) * WIDTH, WIDTH)]

    def out_dst(kind, i):
        ref = (att_out, dq_out, dk_out, dv_out)[kind]
        return ref.at[:, cols(i, WIDTH if kind >= 2 else group_cols)]

    def out_copy(kind, d):
        peer = lax.rem(g + d, heads)
        return pltpu.make_async_remote_copy(
            src_ref=out_src(kind, peer),
            dst_ref=out_dst(kind, g),
            send_sem=out_send.at[kind, d - 1],
            recv_sem=out_recv.at[kind, d - 1],
            device_id=(u, peer),
            device_id_type=MESH,
        )

    def out_arrival(kind, d):
        peer = lax.rem(g + heads - d, heads)
        return pltpu.make_async_remote_copy(
            src_ref=out_dst(kind, peer),
            dst_ref=out_dst(kind, peer),
            send_sem=out_send.at[kind, d - 1],
            recv_sem=out_recv.at[kind, d - 1],
            device_id=(u, peer),
            device_id_type=MESH,
        )

    def own_out(kind):
        return pltpu.make_async_copy(out_src(kind, g), out_dst(kind, g), local_sem.at[4 + kind])

    def send_out(kind):
        for d in range(1, heads):
            out_copy(kind, d).start()
        own_out(kind).start()

    send_out(0)
    norm_copy = pltpu.make_async_copy(norm_buf, norm_out, local_sem.at[8])
    norm_copy.start()

    own_copies[3].wait()
    for d in range(1, heads):
        in_arrival(3, d).wait_recv()

    for h in range(per_group):
        at = slice(h * WIDTH, (h + 1) * WIDTH)
        grad_probs = dot(values, g_buf[:, at], NT)
        p = probs[:, h * block : (h + 1) * block].astype(jnp.float32)
        delta = jnp.sum(p * grad_probs, axis=0, keepdims=True)
        dscores[:, h * block : (h + 1) * block] = (p * (grad_probs - delta) * scale).astype(
            jnp.bfloat16
        )

    def stacked(ref):
        return jnp.concatenate(
            [ref[:, h * WIDTH : (h + 1) * WIDTH] for h in range(per_group)], axis=0
        )

    queries = stacked(q_buf)
    grads = stacked(g_buf)

    def back_copy(k, to):
        return pltpu.make_async_remote_copy(
            src_ref=dkv_send.at[k - 1],
            dst_ref=dkv_recv.at[k - 1],
            send_sem=back_send.at[k - 1],
            recv_sem=back_recv.at[k - 1],
            device_id=(to, g),
            device_id_type=MESH,
        )

    for k in range(reach - 1, -1, -1):
        part = slice((last - k) * block, (last - k + 1) * block)
        dk = dot(dscores[part, :], queries, NN)
        dv = dot(probs[part, :], grads, NN)
        if k == 0:
            dkv_own[:, :WIDTH] = dk
            dkv_own[:, WIDTH:] = dv
        else:
            dkv_send[k - 1, :, :WIDTH] = dk.astype(jnp.bfloat16)
            dkv_send[k - 1, :, WIDTH:] = dv.astype(jnp.bfloat16)

            @pl.when(u - k >= 0)
            def _():
                back_copy(k, u - k).start()

    for h in range(per_group):
        at = slice(h * WIDTH, (h + 1) * WIDTH)
        ds = dscores[:, h * block : (h + 1) * block]
        dq_buf[:, at] = dot(ds, keys, TN).astype(jnp.bfloat16)
    send_out(1)

    for k in range(1, reach):
        @pl.when(u + k < ctxs)
        def _():
            back_copy(k, u + k).wait_recv()

    total = dkv_own[...]
    for k in range(1, reach):
        total = total + dkv_recv[k - 1].astype(jnp.float32)
    dkv_fin[...] = total.astype(jnp.bfloat16)
    send_out(2)
    send_out(3)

    for kind in range(4):
        for d in range(1, heads):
            in_copy(kind, d).wait_send()
    for k in range(1, reach):
        @pl.when(u + k < ctxs)
        def _():
            ctx_copy(k, u + k).wait_send()

        @pl.when(u - k >= 0)
        def _():
            back_copy(k, u - k).wait_send()

    norm_copy.wait()
    for kind in range(4):
        own_out(kind).wait()
        for d in range(1, heads):
            out_copy(kind, d).wait_send()
            out_arrival(kind, d).wait_recv()


def solution(mesh):
    ctxs, heads = mesh.shape["ctx"], mesh.shape["head"]
    reach = min(16, ctxs // 2)

    def step(q, k, v, g, doc_lengths):
        tok = q.shape[0]
        block = tok * heads
        group_cols = q.shape[1] // heads
        per_group = group_cols // WIDTH
        window = reach * block
        bf16, f32 = jnp.bfloat16, jnp.float32
        hbm = pl.BlockSpec(memory_space=pl.ANY)
        dma = pltpu.SemaphoreType.DMA
        return pl.pallas_call(
            functools.partial(kernel, ctxs, heads, reach),
            out_shape=(
                jax.ShapeDtypeStruct(q.shape, bf16),
                jax.ShapeDtypeStruct((per_group, block), f32),
                jax.ShapeDtypeStruct(q.shape, bf16),
                jax.ShapeDtypeStruct(k.shape, bf16),
                jax.ShapeDtypeStruct(k.shape, bf16),
            ),
            in_specs=[hbm] * 4 + [pl.BlockSpec(memory_space=pltpu.SMEM)],
            out_specs=(hbm,) * 5,
            scratch_shapes=[
                pltpu.VMEM((block, group_cols), bf16),
                pltpu.VMEM((block, group_cols), bf16),
                pltpu.VMEM((reach, block, 2 * WIDTH), bf16),
                pltpu.VMEM((window, block), f32),
                pltpu.VMEM((window, per_group * block), bf16),
                pltpu.VMEM((window, per_group * block), bf16),
                pltpu.VMEM((block, group_cols), bf16),
                pltpu.VMEM((block, group_cols), bf16),
                pltpu.VMEM((block, 2 * WIDTH), f32),
                pltpu.VMEM((reach - 1, block, 2 * WIDTH), bf16),
                pltpu.VMEM((reach - 1, block, 2 * WIDTH), bf16),
                pltpu.VMEM((block, 2 * WIDTH), bf16),
                pltpu.VMEM((per_group, block), f32),
                dma((4, heads - 1)),
                dma((4, heads - 1)),
                dma((reach - 1,)),
                dma((reach - 1,)),
                dma((4, heads - 1)),
                dma((4, heads - 1)),
                dma((reach - 1,)),
                dma((reach - 1,)),
                dma((9,)),
            ],
            compiler_params=pltpu.CompilerParams(
                collective_id=0, has_side_effects=True, vmem_limit_bytes=40 * 1024 * 1024
            ),
        )(q, k, v, g, doc_lengths)

    placed = P(("ctx", "head"), None)
    return jax.shard_map(
        step,
        mesh=mesh,
        in_specs=(placed,) * 4 + (P(),),
        out_specs=(placed, P("head", "ctx"), placed, placed, placed),
        check_vma=False,
    )
```

```python
import functools
import math

import jax
import jax.numpy as jnp
from jax import lax
from jax.experimental import pallas as pl
from jax.experimental.pallas import tpu as pltpu
from jax.sharding import PartitionSpec as P

WIDTH = 128
MESH = pl.DeviceIdType.MESH
FILL = -1e30
NT = (((1,), (1,)), ((), ()))
TN = (((0,), (0,)), ((), ()))
NN = (((1,), (0,)), ((), ()))


def dot(a, b, dims):
    return lax.dot_general(a, b, dims, preferred_element_type=jnp.float32)


def kernel(
    ctxs,
    heads,
    reach,
    q_ref,
    k_ref,
    v_ref,
    g_ref,
    doc_ref,
    att_out,
    norm_out,
    dq_out,
    dk_out,
    dv_out,
    q_buf,
    g_buf,
    kv_buf,
    bias,
    probs,
    dscores,
    att_buf,
    dq_buf,
    dkv_own,
    dkv_send,
    dkv_recv,
    dkv_fin,
    norm_buf,
    in_send,
    in_recv,
    ctx_send,
    ctx_recv,
    out_send,
    out_recv,
    back_send,
    back_recv,
    doc_smem,
    local_sem,
):
    u = lax.axis_index("ctx")
    g = lax.axis_index("head")
    tok = q_ref.shape[0]
    block = tok * heads
    group_cols = q_ref.shape[1] // heads
    per_group = group_cols // WIDTH
    window = reach * block
    scale = 1.0 / math.sqrt(WIDTH)
    last = reach - 1

    def rows(i):
        return pl.ds(pl.multiple_of(i * tok, tok), tok)

    def cols(i, width):
        return pl.ds(pl.multiple_of(i * width, width), width)

    barrier = pltpu.get_barrier_semaphore()
    for d in range(1, heads):
        pl.semaphore_signal(
            barrier, inc=1, device_id=(u, lax.rem(g + d, heads)), device_id_type=MESH
        )
    for k in range(1, reach):
        @pl.when(u + k < ctxs)
        def _():
            pl.semaphore_signal(barrier, inc=1, device_id=(u + k, g), device_id_type=MESH)

        @pl.when(u - k >= 0)
        def _():
            pl.semaphore_signal(barrier, inc=1, device_id=(u - k, g), device_id_type=MESH)

    own = [
        (k_ref.at[:, cols(g, WIDTH)], kv_buf.at[last, rows(g), pl.ds(0, WIDTH)]),
        (v_ref.at[:, cols(g, WIDTH)], kv_buf.at[last, rows(g), pl.ds(WIDTH, WIDTH)]),
        (q_ref.at[:, cols(g, group_cols)], q_buf.at[rows(g), :]),
        (g_ref.at[:, cols(g, group_cols)], g_buf.at[rows(g), :]),
    ]
    own_copies = [
        pltpu.make_async_copy(src, dst, local_sem.at[i]) for i, (src, dst) in enumerate(own)
    ]
    doc_copy = pltpu.make_async_copy(doc_ref, doc_smem, local_sem.at[9])
    doc_copy.start()
    for copy in own_copies:
        copy.start()

    for k in range(1, reach):
        @pl.when(u - k < 0)
        def _():
            kv_buf[last - k] = jnp.zeros((block, 2 * WIDTH), jnp.bfloat16)

        @pl.when(u + k >= ctxs)
        def _():
            dkv_recv[k - 1] = jnp.zeros((block, 2 * WIDTH), jnp.bfloat16)

    pl.semaphore_wait(
        barrier,
        (heads - 1) + jnp.minimum(u, reach - 1) + jnp.minimum(ctxs - 1 - u, reach - 1),
    )

    def in_src(kind, i):
        ref = (k_ref, v_ref, q_ref, g_ref)[kind]
        return ref.at[:, cols(i, WIDTH if kind < 2 else group_cols)]

    def in_dst(kind, i):
        if kind < 2:
            return kv_buf.at[last, rows(i), pl.ds(kind * WIDTH, WIDTH)]
        return (q_buf, g_buf)[kind - 2].at[rows(i), :]

    def in_copy(kind, d):
        peer = lax.rem(g + d, heads)
        return pltpu.make_async_remote_copy(
            src_ref=in_src(kind, peer),
            dst_ref=in_dst(kind, g),
            send_sem=in_send.at[kind, d - 1],
            recv_sem=in_recv.at[kind, d - 1],
            device_id=(u, peer),
            device_id_type=MESH,
        )

    def in_arrival(kind, d):
        peer = lax.rem(g + heads - d, heads)
        return pltpu.make_async_remote_copy(
            src_ref=in_dst(kind, peer),
            dst_ref=in_dst(kind, peer),
            send_sem=in_send.at[kind, d - 1],
            recv_sem=in_recv.at[kind, d - 1],
            device_id=(u, peer),
            device_id_type=MESH,
        )

    for kind in range(4):
        for d in range(1, heads):
            in_copy(kind, d).start()

    query_pos = u * block + lax.broadcasted_iota(jnp.int32, (1, block), 1)
    doc_copy.wait()
    begins = jnp.zeros((1, block), jnp.int32)
    bound = jnp.int32(0)
    for j in range(doc_smem.shape[0]):
        bound = bound + doc_smem[j]
        begins = jnp.where(query_pos >= bound, bound, begins)
    key_pos = (u - last) * block + lax.broadcasted_iota(jnp.int32, (window, block), 0)
    bias[...] = jnp.where((key_pos >= begins) & (key_pos <= query_pos), 0.0, FILL)

    own_copies[0].wait()
    own_copies[1].wait()
    for kind in range(2):
        for d in range(1, heads):
            in_arrival(kind, d).wait_recv()

    def ctx_copy(k, to):
        return pltpu.make_async_remote_copy(
            src_ref=kv_buf.at[last],
            dst_ref=kv_buf.at[last - k],
            send_sem=ctx_send.at[k - 1],
            recv_sem=ctx_recv.at[k - 1],
            device_id=(to, g),
            device_id_type=MESH,
        )

    for k in range(1, reach):
        @pl.when(u + k < ctxs)
        def _():
            ctx_copy(k, u + k).start()

    own_copies[2].wait()
    for d in range(1, heads):
        in_arrival(2, d).wait_recv()
    for k in range(1, reach):
        @pl.when(u - k >= 0)
        def _():
            ctx_copy(k, u - k).wait_recv()

    keys = kv_buf[:, :, :WIDTH].reshape(window, WIDTH)
    values = kv_buf[:, :, WIDTH:].reshape(window, WIDTH)

    factor = scale * math.log2(math.e)
    for h in range(per_group):
        at = slice(h * WIDTH, (h + 1) * WIDTH)
        scores = dot(keys, q_buf[:, at], NT) + bias[...]
        top = jnp.max(scores, axis=0, keepdims=True)
        weights = jnp.exp2((scores - top) * factor)
        total = jnp.sum(weights, axis=0, keepdims=True)
        norm_buf[h : h + 1, :] = top * scale + jnp.log(total)
        p = (weights * (1.0 / total)).astype(jnp.bfloat16)
        probs[:, h * block : (h + 1) * block] = p
        att_buf[:, at] = dot(p, values, TN).astype(jnp.bfloat16)

    def out_src(kind, i):
        if kind < 2:
            return (att_buf, dq_buf)[kind].at[rows(i), :]
        return dkv_fin.at[rows(i), pl.ds((kind - 2) * WIDTH, WIDTH)]

    def out_dst(kind, i):
        ref = (att_out, dq_out, dk_out, dv_out)[kind]
        return ref.at[:, cols(i, WIDTH if kind >= 2 else group_cols)]

    def out_copy(kind, d):
        peer = lax.rem(g + d, heads)
        return pltpu.make_async_remote_copy(
            src_ref=out_src(kind, peer),
            dst_ref=out_dst(kind, g),
            send_sem=out_send.at[kind, d - 1],
            recv_sem=out_recv.at[kind, d - 1],
            device_id=(u, peer),
            device_id_type=MESH,
        )

    def out_arrival(kind, d):
        peer = lax.rem(g + heads - d, heads)
        return pltpu.make_async_remote_copy(
            src_ref=out_dst(kind, peer),
            dst_ref=out_dst(kind, peer),
            send_sem=out_send.at[kind, d - 1],
            recv_sem=out_recv.at[kind, d - 1],
            device_id=(u, peer),
            device_id_type=MESH,
        )

    def own_out(kind):
        return pltpu.make_async_copy(out_src(kind, g), out_dst(kind, g), local_sem.at[4 + kind])

    def send_out(kind):
        for d in range(1, heads):
            out_copy(kind, d).start()
        own_out(kind).start()

    send_out(0)
    norm_copy = pltpu.make_async_copy(norm_buf, norm_out, local_sem.at[8])
    norm_copy.start()

    own_copies[3].wait()
    for d in range(1, heads):
        in_arrival(3, d).wait_recv()

    for h in range(per_group):
        at = slice(h * WIDTH, (h + 1) * WIDTH)
        grad_probs = dot(values, g_buf[:, at], NT)
        p = probs[:, h * block : (h + 1) * block].astype(jnp.float32)
        delta = jnp.sum(p * grad_probs, axis=0, keepdims=True)
        dscores[:, h * block : (h + 1) * block] = (p * (grad_probs - delta) * scale).astype(
            jnp.bfloat16
        )

    def stacked(ref):
        return jnp.concatenate(
            [ref[:, h * WIDTH : (h + 1) * WIDTH] for h in range(per_group)], axis=0
        )

    queries = stacked(q_buf)
    grads = stacked(g_buf)

    def back_copy(k, to):
        return pltpu.make_async_remote_copy(
            src_ref=dkv_send.at[k - 1],
            dst_ref=dkv_recv.at[k - 1],
            send_sem=back_send.at[k - 1],
            recv_sem=back_recv.at[k - 1],
            device_id=(to, g),
            device_id_type=MESH,
        )

    for k in range(reach - 1, -1, -1):
        part = slice((last - k) * block, (last - k + 1) * block)
        dk = dot(dscores[part, :], queries, NN)
        dv = dot(probs[part, :], grads, NN)
        if k == 0:
            dkv_own[:, :WIDTH] = dk
            dkv_own[:, WIDTH:] = dv
        else:
            dkv_send[k - 1, :, :WIDTH] = dk.astype(jnp.bfloat16)
            dkv_send[k - 1, :, WIDTH:] = dv.astype(jnp.bfloat16)

            @pl.when(u - k >= 0)
            def _():
                back_copy(k, u - k).start()

    for h in range(per_group):
        at = slice(h * WIDTH, (h + 1) * WIDTH)
        ds = dscores[:, h * block : (h + 1) * block]
        dq_buf[:, at] = dot(ds, keys, TN).astype(jnp.bfloat16)
    send_out(1)

    for k in range(1, reach):
        @pl.when(u + k < ctxs)
        def _():
            back_copy(k, u + k).wait_recv()

    total = dkv_own[...]
    for k in range(1, reach):
        total = total + dkv_recv[k - 1].astype(jnp.float32)
    dkv_fin[...] = total.astype(jnp.bfloat16)
    send_out(2)
    send_out(3)

    for kind in range(4):
        for d in range(1, heads):
            in_copy(kind, d).wait_send()
    for k in range(1, reach):
        @pl.when(u + k < ctxs)
        def _():
            ctx_copy(k, u + k).wait_send()

        @pl.when(u - k >= 0)
        def _():
            back_copy(k, u - k).wait_send()

    norm_copy.wait()
    for kind in range(4):
        own_out(kind).wait()
        for d in range(1, heads):
            out_copy(kind, d).wait_send()
            out_arrival(kind, d).wait_recv()


def place(*refs):
    sources, targets, sem = refs[:5], refs[5:10], refs[10]
    copies = [pltpu.make_async_copy(a, b, sem.at[i]) for i, (a, b) in enumerate(zip(sources, targets))]
    for copy in copies:
        copy.start()
    for copy in copies:
        copy.wait()


def solution(mesh):
    ctxs, heads = mesh.shape["ctx"], mesh.shape["head"]
    reach = min(16, ctxs // 2)

    def step(*arrays):
        q, k, v, g, doc_lengths = (pltpu.with_memory_space_constraint(a, pltpu.HBM) for a in arrays)
        tok = q.shape[0]
        block = tok * heads
        group_cols = q.shape[1] // heads
        per_group = group_cols // WIDTH
        window = reach * block
        bf16, f32 = jnp.bfloat16, jnp.float32
        any_space = pl.BlockSpec(memory_space=pl.ANY)
        hbm = pl.BlockSpec(memory_space=pltpu.HBM)
        dma = pltpu.SemaphoreType.DMA
        results = pl.pallas_call(
            functools.partial(kernel, ctxs, heads, reach),
            out_shape=(
                pltpu.VMEM(q.shape, bf16),
                pltpu.VMEM((per_group, block), f32),
                pltpu.VMEM(q.shape, bf16),
                pltpu.VMEM(k.shape, bf16),
                pltpu.VMEM(k.shape, bf16),
            ),
            in_specs=[hbm] * 5,
            out_specs=(any_space,) * 5,
            scratch_shapes=[
                pltpu.VMEM((block, group_cols), bf16),
                pltpu.VMEM((block, group_cols), bf16),
                pltpu.VMEM((reach, block, 2 * WIDTH), bf16),
                pltpu.VMEM((window, block), f32),
                pltpu.VMEM((window, per_group * block), bf16),
                pltpu.VMEM((window, per_group * block), bf16),
                pltpu.VMEM((block, group_cols), bf16),
                pltpu.VMEM((block, group_cols), bf16),
                pltpu.VMEM((block, 2 * WIDTH), f32),
                pltpu.VMEM((reach - 1, block, 2 * WIDTH), bf16),
                pltpu.VMEM((reach - 1, block, 2 * WIDTH), bf16),
                pltpu.VMEM((block, 2 * WIDTH), bf16),
                pltpu.VMEM((per_group, block), f32),
                dma((4, heads - 1)),
                dma((4, heads - 1)),
                dma((reach - 1,)),
                dma((reach - 1,)),
                dma((4, heads - 1)),
                dma((4, heads - 1)),
                dma((reach - 1,)),
                dma((reach - 1,)),
                pltpu.SMEM(doc_lengths.shape, jnp.int32),
                dma((10,)),
            ],
            compiler_params=pltpu.CompilerParams(
                collective_id=0, has_side_effects=True, vmem_limit_bytes=40 * 1024 * 1024
            ),
        )(q, k, v, g, doc_lengths)
        return pl.pallas_call(
            place,
            out_shape=tuple(jax.ShapeDtypeStruct(r.shape, r.dtype) for r in results),
            in_specs=[any_space] * 5,
            out_specs=(hbm,) * 5,
            scratch_shapes=[dma((5,))],
            compiler_params=pltpu.CompilerParams(vmem_limit_bytes=40 * 1024 * 1024),
        )(*results)

    placed = P(("ctx", "head"), None)
    return jax.shard_map(
        step,
        mesh=mesh,
        in_specs=(placed,) * 4 + (P(),),
        out_specs=(placed, P("head", "ctx"), placed, placed, placed),
        check_vma=False,
    )
```

```python
import functools
import math

import jax
import jax.numpy as jnp
from jax import lax
from jax.experimental import pallas as pl
from jax.experimental.pallas import tpu as pltpu
from jax.sharding import PartitionSpec as P

WIDTH = 128
MESH = pl.DeviceIdType.MESH
FILL = -1e30
NT = (((1,), (1,)), ((), ()))
TN = (((0,), (0,)), ((), ()))
NN = (((1,), (0,)), ((), ()))


def dot(a, b, dims):
    return lax.dot_general(a, b, dims, preferred_element_type=jnp.float32)


def kernel(
    ctxs,
    heads,
    reach,
    q_ref,
    k_ref,
    v_ref,
    g_ref,
    doc_ref,
    att_out,
    norm_out,
    dq_out,
    dk_out,
    dv_out,
    q_buf,
    g_buf,
    kv_buf,
    bias,
    probs,
    dscores,
    att_buf,
    dq_buf,
    dk_own,
    dv_send,
    dv_recv,
    dk_send,
    dk_recv,
    dkv_fin,
    norm_buf,
    in_send,
    in_recv,
    ctx_send,
    ctx_recv,
    out_send,
    out_recv,
    back_send,
    back_recv,
    dv_sems,
    doc_smem,
    local_sem,
):
    u = lax.axis_index("ctx")
    g = lax.axis_index("head")
    tok = q_ref.shape[0]
    block = tok * heads
    group_cols = q_ref.shape[1] // heads
    per_group = group_cols // WIDTH
    window = reach * block
    scale = 1.0 / math.sqrt(WIDTH)
    last = reach - 1

    def rows(i):
        return pl.ds(pl.multiple_of(i * tok, tok), tok)

    def cols(i, width):
        return pl.ds(pl.multiple_of(i * width, width), width)

    pairs = heads // 2
    far_first = list(range(2, heads)) + [1]

    def to_peer(d):
        return lax.rem(g // 2 + d // 2, pairs) * 2 + lax.rem(lax.rem(g, 2) + d % 2, 2)

    def from_peer(d):
        return lax.rem(g // 2 + pairs - d // 2, pairs) * 2 + lax.rem(lax.rem(g, 2) + d % 2, 2)

    barrier = pltpu.get_barrier_semaphore()
    for d in range(1, heads):
        pl.semaphore_signal(
            barrier, inc=1, device_id=(u, to_peer(d)), device_id_type=MESH
        )
    for k in range(1, reach):
        @pl.when(u + k < ctxs)
        def _():
            pl.semaphore_signal(barrier, inc=1, device_id=(u + k, g), device_id_type=MESH)

        @pl.when(u - k >= 0)
        def _():
            pl.semaphore_signal(barrier, inc=1, device_id=(u - k, g), device_id_type=MESH)

    own = [
        (k_ref.at[:, cols(g, WIDTH)], kv_buf.at[last, rows(g), pl.ds(0, WIDTH)]),
        (v_ref.at[:, cols(g, WIDTH)], kv_buf.at[last, rows(g), pl.ds(WIDTH, WIDTH)]),
        (q_ref.at[:, cols(g, group_cols)], q_buf.at[rows(g), :]),
        (g_ref.at[:, cols(g, group_cols)], g_buf.at[rows(g), :]),
    ]
    own_copies = [
        pltpu.make_async_copy(src, dst, local_sem.at[i]) for i, (src, dst) in enumerate(own)
    ]
    doc_copy = pltpu.make_async_copy(doc_ref, doc_smem, local_sem.at[9])
    doc_copy.start()
    for copy in own_copies:
        copy.start()

    for k in range(1, reach):
        @pl.when(u - k < 0)
        def _():
            kv_buf[last - k] = jnp.zeros((block, 2 * WIDTH), jnp.bfloat16)

        @pl.when(u + k >= ctxs)
        def _():
            dv_recv[k - 1] = jnp.zeros((block, WIDTH), jnp.bfloat16)
            dk_recv[k - 1] = jnp.zeros((heads, tok, WIDTH), jnp.bfloat16)

    pl.semaphore_wait(
        barrier,
        (heads - 1) + jnp.minimum(u, reach - 1) + jnp.minimum(ctxs - 1 - u, reach - 1),
    )

    def in_src(kind, i):
        ref = (k_ref, v_ref, q_ref, g_ref)[kind]
        return ref.at[:, cols(i, WIDTH if kind < 2 else group_cols)]

    def in_dst(kind, i):
        if kind < 2:
            return kv_buf.at[last, rows(i), pl.ds(kind * WIDTH, WIDTH)]
        return (q_buf, g_buf)[kind - 2].at[rows(i), :]

    def in_copy(kind, d):
        peer = to_peer(d)
        return pltpu.make_async_remote_copy(
            src_ref=in_src(kind, peer),
            dst_ref=in_dst(kind, g),
            send_sem=in_send.at[kind, d - 1],
            recv_sem=in_recv.at[kind, d - 1],
            device_id=(u, peer),
            device_id_type=MESH,
        )

    def in_arrival(kind, d):
        peer = from_peer(d)
        return pltpu.make_async_remote_copy(
            src_ref=in_dst(kind, peer),
            dst_ref=in_dst(kind, peer),
            send_sem=in_send.at[kind, d - 1],
            recv_sem=in_recv.at[kind, d - 1],
            device_id=(u, peer),
            device_id_type=MESH,
        )

    for kind in range(4):
        for d in far_first:
            in_copy(kind, d).start()

    def ctx_copy(k, d, to):
        piece = rows(from_peer(d))
        return pltpu.make_async_remote_copy(
            src_ref=kv_buf.at[last, piece, :],
            dst_ref=kv_buf.at[last - k, piece, :],
            send_sem=ctx_send.at[k - 1, d],
            recv_sem=ctx_recv.at[k - 1, d],
            device_id=(to, g),
            device_id_type=MESH,
        )

    for d in range(heads):
        for kind in range(2):
            if d == 0:
                own_copies[kind].wait()
            else:
                in_arrival(kind, d).wait_recv()
        for k in range(reach - 1, 0, -1):
            @pl.when(u + k < ctxs)
            def _():
                ctx_copy(k, d, u + k).start()

    query_pos = u * block + lax.broadcasted_iota(jnp.int32, (1, block), 1)
    doc_copy.wait()
    begins = jnp.zeros((1, block), jnp.int32)
    bound = jnp.int32(0)
    for j in range(doc_smem.shape[0]):
        bound = bound + doc_smem[j]
        begins = jnp.where(query_pos >= bound, bound, begins)
    key_pos = (u - last) * block + lax.broadcasted_iota(jnp.int32, (window, block), 0)
    bias[...] = jnp.where((key_pos >= begins) & (key_pos <= query_pos), 0.0, FILL)

    own_copies[2].wait()
    for d in range(1, heads):
        in_arrival(2, d).wait_recv()
    for k in range(1, reach):
        @pl.when(u - k >= 0)
        def _():
            for d in range(heads):
                ctx_copy(k, d, u - k).wait_recv()

    keys = kv_buf[:, :, :WIDTH].reshape(window, WIDTH)
    values = kv_buf[:, :, WIDTH:].reshape(window, WIDTH)

    factor = scale * math.log2(math.e)
    for h in range(per_group):
        at = slice(h * WIDTH, (h + 1) * WIDTH)
        scores = dot(keys, q_buf[:, at], NT) + bias[...]
        top = jnp.max(scores, axis=0, keepdims=True)
        weights = jnp.exp2((scores - top) * factor)
        total = jnp.sum(weights, axis=0, keepdims=True)
        norm_buf[h : h + 1, :] = top * scale + jnp.log(total)
        p = (weights * (1.0 / total)).astype(jnp.bfloat16)
        probs[:, h * block : (h + 1) * block] = p
        att_buf[:, at] = dot(p, values, TN).astype(jnp.bfloat16)

    def out_src(kind, i):
        if kind < 2:
            return (att_buf, dq_buf)[kind].at[rows(i), :]
        return dkv_fin.at[kind - 2, rows(i), :]

    def out_dst(kind, i):
        ref = (att_out, dq_out, dk_out, dv_out)[kind]
        return ref.at[:, cols(i, WIDTH if kind >= 2 else group_cols)]

    def out_copy(kind, d):
        peer = to_peer(d)
        return pltpu.make_async_remote_copy(
            src_ref=out_src(kind, peer),
            dst_ref=out_dst(kind, g),
            send_sem=out_send.at[kind, d - 1],
            recv_sem=out_recv.at[kind, d - 1],
            device_id=(u, peer),
            device_id_type=MESH,
        )

    def out_arrival(kind, d):
        peer = from_peer(d)
        return pltpu.make_async_remote_copy(
            src_ref=out_dst(kind, peer),
            dst_ref=out_dst(kind, peer),
            send_sem=out_send.at[kind, d - 1],
            recv_sem=out_recv.at[kind, d - 1],
            device_id=(u, peer),
            device_id_type=MESH,
        )

    def own_out(kind):
        return pltpu.make_async_copy(out_src(kind, g), out_dst(kind, g), local_sem.at[4 + kind])

    def send_out(kind):
        for d in far_first:
            out_copy(kind, d).start()
        own_out(kind).start()

    send_out(0)
    norm_copy = pltpu.make_async_copy(norm_buf, norm_out, local_sem.at[8])
    norm_copy.start()

    own_copies[3].wait()
    for d in range(1, heads):
        in_arrival(3, d).wait_recv()

    def stacked(ref):
        return jnp.concatenate(
            [ref[:, h * WIDTH : (h + 1) * WIDTH] for h in range(per_group)], axis=0
        )

    def dv_copy(k, to):
        return pltpu.make_async_remote_copy(
            src_ref=dv_send.at[k - 1],
            dst_ref=dv_recv.at[k - 1],
            send_sem=dv_sems.at[0, k - 1],
            recv_sem=dv_sems.at[1, k - 1],
            device_id=(to, g),
            device_id_type=MESH,
        )

    def dk_copy(k, d, to):
        return pltpu.make_async_remote_copy(
            src_ref=dk_send.at[k - 1, rows(to_peer(d)), :],
            dst_ref=dk_recv.at[k - 1, d],
            send_sem=back_send.at[k - 1, d],
            recv_sem=back_recv.at[k - 1, d],
            device_id=(to, g),
            device_id_type=MESH,
        )

    def part(k):
        return slice((last - k) * block, (last - k + 1) * block)

    grads = stacked(g_buf)
    for k in range(reach - 1, 0, -1):
        dv_send[k - 1] = dot(probs[part(k), :], grads, NN).astype(jnp.bfloat16)

        @pl.when(u - k >= 0)
        def _():
            dv_copy(k, u - k).start()

    for h in range(per_group):
        at = slice(h * WIDTH, (h + 1) * WIDTH)
        grad_probs = dot(values, g_buf[:, at], NT)
        p = probs[:, h * block : (h + 1) * block].astype(jnp.float32)
        delta = jnp.sum(p * grad_probs, axis=0, keepdims=True)
        dscores[:, h * block : (h + 1) * block] = (p * (grad_probs - delta) * scale).astype(
            jnp.bfloat16
        )

    queries = stacked(q_buf)
    for k in range(reach - 1, 0, -1):
        dk_send[k - 1] = dot(dscores[part(k), :], queries, NN).astype(jnp.bfloat16)

        @pl.when(u - k >= 0)
        def _():
            for d in far_first + [0]:
                dk_copy(k, d, u - k).start()

    for h in range(per_group):
        at = slice(h * WIDTH, (h + 1) * WIDTH)
        ds = dscores[:, h * block : (h + 1) * block]
        dq_buf[:, at] = dot(ds, keys, TN).astype(jnp.bfloat16)
    send_out(1)

    dv_total = dot(probs[part(0), :], grads, NN)
    dk_own[...] = dot(dscores[part(0), :], queries, NN)

    for k in range(1, reach):
        @pl.when(u + k < ctxs)
        def _():
            dv_copy(k, u + k).wait_recv()

        dv_total = dv_total + dv_recv[k - 1].astype(jnp.float32)
    dkv_fin[1] = dv_total.astype(jnp.bfloat16)
    send_out(3)

    for d in far_first + [0]:
        piece = rows(to_peer(d))
        total = dk_own[piece, :]
        for k in range(1, reach):
            @pl.when(u + k < ctxs)
            def _():
                dk_copy(k, d, u + k).wait_recv()

            total = total + dk_recv[k - 1, d].astype(jnp.float32)
        dkv_fin[0, piece, :] = total.astype(jnp.bfloat16)
        if d == 0:
            own_out(2).start()
        else:
            out_copy(2, d).start()

    for kind in range(4):
        for d in range(1, heads):
            in_copy(kind, d).wait_send()
    for k in range(1, reach):
        @pl.when(u + k < ctxs)
        def _():
            for d in range(heads):
                ctx_copy(k, d, u + k).wait_send()

        @pl.when(u - k >= 0)
        def _():
            dv_copy(k, u - k).wait_send()
            for d in range(heads):
                dk_copy(k, d, u - k).wait_send()

    norm_copy.wait()
    for kind in range(4):
        own_out(kind).wait()
        for d in range(1, heads):
            out_copy(kind, d).wait_send()
            out_arrival(kind, d).wait_recv()


def place(*refs):
    sources, targets, sem = refs[:5], refs[5:10], refs[10]
    copies = [pltpu.make_async_copy(a, b, sem.at[i]) for i, (a, b) in enumerate(zip(sources, targets))]
    for copy in copies:
        copy.start()
    for copy in copies:
        copy.wait()


def solution(mesh):
    ctxs, heads = mesh.shape["ctx"], mesh.shape["head"]
    reach = min(16, ctxs // 2)

    def step(*arrays):
        q, k, v, g, doc_lengths = (pltpu.with_memory_space_constraint(a, pltpu.HBM) for a in arrays)
        tok = q.shape[0]
        block = tok * heads
        group_cols = q.shape[1] // heads
        per_group = group_cols // WIDTH
        window = reach * block
        bf16, f32 = jnp.bfloat16, jnp.float32
        any_space = pl.BlockSpec(memory_space=pl.ANY)
        hbm = pl.BlockSpec(memory_space=pltpu.HBM)
        dma = pltpu.SemaphoreType.DMA
        results = pl.pallas_call(
            functools.partial(kernel, ctxs, heads, reach),
            out_shape=(
                pltpu.VMEM(q.shape, bf16),
                pltpu.VMEM((per_group, block), f32),
                pltpu.VMEM(q.shape, bf16),
                pltpu.VMEM(k.shape, bf16),
                pltpu.VMEM(k.shape, bf16),
            ),
            in_specs=[hbm] * 5,
            out_specs=(any_space,) * 5,
            scratch_shapes=[
                pltpu.VMEM((block, group_cols), bf16),
                pltpu.VMEM((block, group_cols), bf16),
                pltpu.VMEM((reach, block, 2 * WIDTH), bf16),
                pltpu.VMEM((window, block), f32),
                pltpu.VMEM((window, per_group * block), bf16),
                pltpu.VMEM((window, per_group * block), bf16),
                pltpu.VMEM((block, group_cols), bf16),
                pltpu.VMEM((block, group_cols), bf16),
                pltpu.VMEM((block, WIDTH), f32),
                pltpu.VMEM((reach - 1, block, WIDTH), bf16),
                pltpu.VMEM((reach - 1, block, WIDTH), bf16),
                pltpu.VMEM((reach - 1, block, WIDTH), bf16),
                pltpu.VMEM((reach - 1, heads, tok, WIDTH), bf16),
                pltpu.VMEM((2, block, WIDTH), bf16),
                pltpu.VMEM((per_group, block), f32),
                dma((4, heads - 1)),
                dma((4, heads - 1)),
                dma((reach - 1, heads)),
                dma((reach - 1, heads)),
                dma((4, heads - 1)),
                dma((4, heads - 1)),
                dma((reach - 1, heads)),
                dma((reach - 1, heads)),
                dma((2, reach - 1)),
                pltpu.SMEM(doc_lengths.shape, jnp.int32),
                dma((10,)),
            ],
            compiler_params=pltpu.CompilerParams(
                collective_id=0, has_side_effects=True, vmem_limit_bytes=40 * 1024 * 1024
            ),
        )(q, k, v, g, doc_lengths)
        return pl.pallas_call(
            place,
            out_shape=tuple(jax.ShapeDtypeStruct(r.shape, r.dtype) for r in results),
            in_specs=[any_space] * 5,
            out_specs=(hbm,) * 5,
            scratch_shapes=[dma((5,))],
            compiler_params=pltpu.CompilerParams(vmem_limit_bytes=40 * 1024 * 1024),
        )(*results)

    placed = P(("ctx", "head"), None)
    return jax.shard_map(
        step,
        mesh=mesh,
        in_specs=(placed,) * 4 + (P(),),
        out_specs=(placed, P("head", "ctx"), placed, placed, placed),
        check_vma=False,
    )
```

```python
import functools
import math

import jax
import jax.numpy as jnp
from jax import lax
from jax.experimental import pallas as pl
from jax.experimental.pallas import tpu as pltpu
from jax.sharding import PartitionSpec as P

WIDTH = 128
MESH = pl.DeviceIdType.MESH
FILL = -1e30
NT = (((1,), (1,)), ((), ()))
TN = (((0,), (0,)), ((), ()))
NN = (((1,), (0,)), ((), ()))


def dot(a, b, dims):
    return lax.dot_general(a, b, dims, preferred_element_type=jnp.float32)


def kernel(
    ctxs,
    heads,
    reach,
    q_ref,
    k_ref,
    v_ref,
    g_ref,
    doc_ref,
    att_out,
    norm_out,
    dq_out,
    dk_out,
    dv_out,
    q_buf,
    g_buf,
    kv_buf,
    bias,
    probs,
    dscores,
    att_buf,
    dq_buf,
    dk_own,
    dv_send,
    dv_recv,
    dk_send,
    dk_recv,
    dkv_fin,
    norm_buf,
    in_send,
    in_recv,
    ctx_send,
    ctx_recv,
    out_send,
    out_recv,
    back_send,
    back_recv,
    dv_sems,
    doc_smem,
    local_sem,
):
    u = lax.axis_index("ctx")
    g = lax.axis_index("head")
    tok = q_ref.shape[0]
    block = tok * heads
    group_cols = q_ref.shape[1] // heads
    per_group = group_cols // WIDTH
    window = reach * block
    scale = 1.0 / math.sqrt(WIDTH)
    last = reach - 1

    def rows(i):
        return pl.ds(pl.multiple_of(i * tok, tok), tok)

    def cols(i, width):
        return pl.ds(pl.multiple_of(i * width, width), width)

    pairs = heads // 2
    far_first = list(range(2, heads)) + [1]

    def to_peer(d):
        return lax.rem(g // 2 + d // 2, pairs) * 2 + lax.rem(lax.rem(g, 2) + d % 2, 2)

    def from_peer(d):
        return lax.rem(g // 2 + pairs - d // 2, pairs) * 2 + lax.rem(lax.rem(g, 2) + d % 2, 2)

    barrier = pltpu.get_barrier_semaphore()
    for d in range(1, heads):
        pl.semaphore_signal(
            barrier, inc=1, device_id=(u, to_peer(d)), device_id_type=MESH
        )
    for k in range(1, reach):
        @pl.when(u + k < ctxs)
        def _():
            pl.semaphore_signal(barrier, inc=1, device_id=(u + k, g), device_id_type=MESH)

        @pl.when(u - k >= 0)
        def _():
            pl.semaphore_signal(barrier, inc=1, device_id=(u - k, g), device_id_type=MESH)

    own = [
        (k_ref.at[:, cols(g, WIDTH)], kv_buf.at[last, rows(g), pl.ds(0, WIDTH)]),
        (v_ref.at[:, cols(g, WIDTH)], kv_buf.at[last, rows(g), pl.ds(WIDTH, WIDTH)]),
        (q_ref.at[:, cols(g, group_cols)], q_buf.at[rows(g), :]),
        (g_ref.at[:, cols(g, group_cols)], g_buf.at[rows(g), :]),
    ]
    own_copies = [
        pltpu.make_async_copy(src, dst, local_sem.at[i]) for i, (src, dst) in enumerate(own)
    ]
    doc_copy = pltpu.make_async_copy(doc_ref, doc_smem, local_sem.at[9])
    doc_copy.start()
    for copy in own_copies:
        copy.start()

    for k in range(1, reach):
        @pl.when(u - k < 0)
        def _():
            kv_buf[last - k] = jnp.zeros((block, 2 * WIDTH), jnp.bfloat16)

        @pl.when(u + k >= ctxs)
        def _():
            dv_recv[k - 1] = jnp.zeros((block, WIDTH), jnp.bfloat16)
            dk_recv[k - 1] = jnp.zeros((heads, tok, WIDTH), jnp.bfloat16)

    pl.semaphore_wait(
        barrier,
        (heads - 1) + jnp.minimum(u, reach - 1) + jnp.minimum(ctxs - 1 - u, reach - 1),
    )

    def in_src(kind, i):
        ref = (k_ref, v_ref, q_ref, g_ref)[kind]
        return ref.at[:, cols(i, WIDTH if kind < 2 else group_cols)]

    def in_dst(kind, i):
        if kind < 2:
            return kv_buf.at[last, rows(i), pl.ds(kind * WIDTH, WIDTH)]
        return (q_buf, g_buf)[kind - 2].at[rows(i), :]

    def in_copy(kind, d):
        peer = to_peer(d)
        return pltpu.make_async_remote_copy(
            src_ref=in_src(kind, peer),
            dst_ref=in_dst(kind, g),
            send_sem=in_send.at[kind, d - 1],
            recv_sem=in_recv.at[kind, d - 1],
            device_id=(u, peer),
            device_id_type=MESH,
        )

    def in_arrival(kind, d):
        peer = from_peer(d)
        return pltpu.make_async_remote_copy(
            src_ref=in_dst(kind, peer),
            dst_ref=in_dst(kind, peer),
            send_sem=in_send.at[kind, d - 1],
            recv_sem=in_recv.at[kind, d - 1],
            device_id=(u, peer),
            device_id_type=MESH,
        )

    for kind in range(4):
        for d in far_first:
            in_copy(kind, d).start()

    def ctx_copy(k, d, to):
        piece = rows(from_peer(d))
        return pltpu.make_async_remote_copy(
            src_ref=kv_buf.at[last, piece, :],
            dst_ref=kv_buf.at[last - k, piece, :],
            send_sem=ctx_send.at[k - 1, d],
            recv_sem=ctx_recv.at[k - 1, d],
            device_id=(to, g),
            device_id_type=MESH,
        )

    for d in range(heads):
        for kind in range(2):
            if d == 0:
                own_copies[kind].wait()
            else:
                in_arrival(kind, d).wait_recv()
        for k in range(reach - 1, 0, -1):
            @pl.when(u + k < ctxs)
            def _():
                ctx_copy(k, d, u + k).start()

    query_pos = u * block + lax.broadcasted_iota(jnp.int32, (1, block), 1)
    doc_copy.wait()
    begins = jnp.zeros((1, block), jnp.int32)
    bound = jnp.int32(0)
    for j in range(doc_smem.shape[0]):
        bound = bound + doc_smem[j]
        begins = jnp.where(query_pos >= bound, bound, begins)
    key_pos = (u - last) * block + lax.broadcasted_iota(jnp.int32, (window, block), 0)
    bias[...] = jnp.where((key_pos >= begins) & (key_pos <= query_pos), 0.0, FILL)

    own_copies[2].wait()
    for d in range(1, heads):
        in_arrival(2, d).wait_recv()
    for k in range(1, reach):
        @pl.when(u - k >= 0)
        def _():
            for d in range(heads):
                ctx_copy(k, d, u - k).wait_recv()

    keys = kv_buf[:, :, :WIDTH].reshape(window, WIDTH)
    values = kv_buf[:, :, WIDTH:].reshape(window, WIDTH)

    factor = scale * math.log2(math.e)
    for h in range(per_group):
        at = slice(h * WIDTH, (h + 1) * WIDTH)
        scores = dot(keys, q_buf[:, at], NT) + bias[...]
        top = jnp.max(scores, axis=0, keepdims=True)
        weights = jnp.exp2((scores - top) * factor)
        total = jnp.sum(weights, axis=0, keepdims=True)
        norm_buf[h : h + 1, :] = top * scale + jnp.log(total)
        p = (weights * (1.0 / total)).astype(jnp.bfloat16)
        probs[:, h * block : (h + 1) * block] = p
        att_buf[:, at] = dot(p, values, TN).astype(jnp.bfloat16)

    def out_src(kind, i):
        if kind < 2:
            return (att_buf, dq_buf)[kind].at[rows(i), :]
        return dkv_fin.at[kind - 2, rows(i), :]

    def out_dst(kind, i):
        ref = (att_out, dq_out, dk_out, dv_out)[kind]
        return ref.at[:, cols(i, WIDTH if kind >= 2 else group_cols)]

    def out_copy(kind, d):
        peer = to_peer(d)
        return pltpu.make_async_remote_copy(
            src_ref=out_src(kind, peer),
            dst_ref=out_dst(kind, g),
            send_sem=out_send.at[kind, d - 1],
            recv_sem=out_recv.at[kind, d - 1],
            device_id=(u, peer),
            device_id_type=MESH,
        )

    def out_arrival(kind, d):
        peer = from_peer(d)
        return pltpu.make_async_remote_copy(
            src_ref=out_dst(kind, peer),
            dst_ref=out_dst(kind, peer),
            send_sem=out_send.at[kind, d - 1],
            recv_sem=out_recv.at[kind, d - 1],
            device_id=(u, peer),
            device_id_type=MESH,
        )

    def own_out(kind):
        return pltpu.make_async_copy(out_src(kind, g), out_dst(kind, g), local_sem.at[4 + kind])

    def send_out(kind):
        for d in far_first:
            out_copy(kind, d).start()
        own_out(kind).start()

    send_out(0)
    norm_copy = pltpu.make_async_copy(norm_buf, norm_out, local_sem.at[8])
    norm_copy.start()

    own_copies[3].wait()
    for d in range(1, heads):
        in_arrival(3, d).wait_recv()

    def stacked(ref):
        return jnp.concatenate(
            [ref[:, h * WIDTH : (h + 1) * WIDTH] for h in range(per_group)], axis=0
        )

    def dv_copy(k, to):
        return pltpu.make_async_remote_copy(
            src_ref=dv_send.at[k - 1],
            dst_ref=dv_recv.at[k - 1],
            send_sem=dv_sems.at[0, k - 1],
            recv_sem=dv_sems.at[1, k - 1],
            device_id=(to, g),
            device_id_type=MESH,
        )

    def dk_copy(k, d, to):
        return pltpu.make_async_remote_copy(
            src_ref=dk_send.at[k - 1, rows(to_peer(d)), :],
            dst_ref=dk_recv.at[k - 1, d],
            send_sem=back_send.at[k - 1, d],
            recv_sem=back_recv.at[k - 1, d],
            device_id=(to, g),
            device_id_type=MESH,
        )

    def part(k):
        return slice((last - k) * block, (last - k + 1) * block)

    grads = stacked(g_buf)
    for k in range(reach - 1, 0, -1):
        dv_send[k - 1] = dot(probs[part(k), :], grads, NN).astype(jnp.bfloat16)

        @pl.when(u - k >= 0)
        def _():
            dv_copy(k, u - k).start()

    for h in range(per_group):
        at = slice(h * WIDTH, (h + 1) * WIDTH)
        grad_probs = dot(values, g_buf[:, at], NT)
        p = probs[:, h * block : (h + 1) * block].astype(jnp.float32)
        delta = jnp.sum(p * grad_probs, axis=0, keepdims=True)
        dscores[:, h * block : (h + 1) * block] = (p * (grad_probs - delta) * scale).astype(
            jnp.bfloat16
        )

    for h in range(per_group):
        at = slice(h * WIDTH, (h + 1) * WIDTH)
        ds = dscores[:, h * block : (h + 1) * block]
        dq_buf[:, at] = dot(ds, keys, TN).astype(jnp.bfloat16)
    send_out(1)

    queries = stacked(q_buf)
    for k in range(reach - 1, 0, -1):
        dk_send[k - 1] = dot(dscores[part(k), :], queries, NN).astype(jnp.bfloat16)

        @pl.when(u - k >= 0)
        def _():
            for d in far_first + [0]:
                dk_copy(k, d, u - k).start()

    dv_total = dot(probs[part(0), :], grads, NN)
    dk_own[...] = dot(dscores[part(0), :], queries, NN)

    for k in range(1, reach):
        @pl.when(u + k < ctxs)
        def _():
            dv_copy(k, u + k).wait_recv()

        dv_total = dv_total + dv_recv[k - 1].astype(jnp.float32)
    dkv_fin[1] = dv_total.astype(jnp.bfloat16)
    send_out(3)

    for d in far_first + [0]:
        piece = rows(to_peer(d))
        total = dk_own[piece, :]
        for k in range(1, reach):
            @pl.when(u + k < ctxs)
            def _():
                dk_copy(k, d, u + k).wait_recv()

            total = total + dk_recv[k - 1, d].astype(jnp.float32)
        dkv_fin[0, piece, :] = total.astype(jnp.bfloat16)
        if d == 0:
            own_out(2).start()
        else:
            out_copy(2, d).start()

    for kind in range(4):
        for d in range(1, heads):
            in_copy(kind, d).wait_send()
    for k in range(1, reach):
        @pl.when(u + k < ctxs)
        def _():
            for d in range(heads):
                ctx_copy(k, d, u + k).wait_send()

        @pl.when(u - k >= 0)
        def _():
            dv_copy(k, u - k).wait_send()
            for d in range(heads):
                dk_copy(k, d, u - k).wait_send()

    norm_copy.wait()
    for kind in range(4):
        own_out(kind).wait()
        for d in range(1, heads):
            out_copy(kind, d).wait_send()
            out_arrival(kind, d).wait_recv()


def place(*refs):
    sources, targets, sem = refs[:5], refs[5:10], refs[10]
    copies = [pltpu.make_async_copy(a, b, sem.at[i]) for i, (a, b) in enumerate(zip(sources, targets))]
    for copy in copies:
        copy.start()
    for copy in copies:
        copy.wait()


def solution(mesh):
    ctxs, heads = mesh.shape["ctx"], mesh.shape["head"]
    reach = min(16, ctxs // 2)

    def step(*arrays):
        q, k, v, g, doc_lengths = (pltpu.with_memory_space_constraint(a, pltpu.HBM) for a in arrays)
        tok = q.shape[0]
        block = tok * heads
        group_cols = q.shape[1] // heads
        per_group = group_cols // WIDTH
        window = reach * block
        bf16, f32 = jnp.bfloat16, jnp.float32
        any_space = pl.BlockSpec(memory_space=pl.ANY)
        hbm = pl.BlockSpec(memory_space=pltpu.HBM)
        dma = pltpu.SemaphoreType.DMA
        results = pl.pallas_call(
            functools.partial(kernel, ctxs, heads, reach),
            out_shape=(
                pltpu.VMEM(q.shape, bf16),
                pltpu.VMEM((per_group, block), f32),
                pltpu.VMEM(q.shape, bf16),
                pltpu.VMEM(k.shape, bf16),
                pltpu.VMEM(k.shape, bf16),
            ),
            in_specs=[hbm] * 5,
            out_specs=(any_space,) * 5,
            scratch_shapes=[
                pltpu.VMEM((block, group_cols), bf16),
                pltpu.VMEM((block, group_cols), bf16),
                pltpu.VMEM((reach, block, 2 * WIDTH), bf16),
                pltpu.VMEM((window, block), f32),
                pltpu.VMEM((window, per_group * block), bf16),
                pltpu.VMEM((window, per_group * block), bf16),
                pltpu.VMEM((block, group_cols), bf16),
                pltpu.VMEM((block, group_cols), bf16),
                pltpu.VMEM((block, WIDTH), f32),
                pltpu.VMEM((reach - 1, block, WIDTH), bf16),
                pltpu.VMEM((reach - 1, block, WIDTH), bf16),
                pltpu.VMEM((reach - 1, block, WIDTH), bf16),
                pltpu.VMEM((reach - 1, heads, tok, WIDTH), bf16),
                pltpu.VMEM((2, block, WIDTH), bf16),
                pltpu.VMEM((per_group, block), f32),
                dma((4, heads - 1)),
                dma((4, heads - 1)),
                dma((reach - 1, heads)),
                dma((reach - 1, heads)),
                dma((4, heads - 1)),
                dma((4, heads - 1)),
                dma((reach - 1, heads)),
                dma((reach - 1, heads)),
                dma((2, reach - 1)),
                pltpu.SMEM(doc_lengths.shape, jnp.int32),
                dma((10,)),
            ],
            compiler_params=pltpu.CompilerParams(
                collective_id=0, has_side_effects=True, vmem_limit_bytes=40 * 1024 * 1024
            ),
        )(q, k, v, g, doc_lengths)
        return pl.pallas_call(
            place,
            out_shape=tuple(jax.ShapeDtypeStruct(r.shape, r.dtype) for r in results),
            in_specs=[any_space] * 5,
            out_specs=(hbm,) * 5,
            scratch_shapes=[dma((5,))],
            compiler_params=pltpu.CompilerParams(vmem_limit_bytes=40 * 1024 * 1024),
        )(*results)

    placed = P(("ctx", "head"), None)
    return jax.shard_map(
        step,
        mesh=mesh,
        in_specs=(placed,) * 4 + (P(),),
        out_specs=(placed, P("head", "ctx"), placed, placed, placed),
        check_vma=False,
    )
```
